32 devices in a mesh: rows: 8 (over y, x, core), cols: 4 (over z).
Axes of the slice: x: 2, y: 2, z: 4, core: 2. Of those that a mesh axis runs over, the one named last changes fastest.
Arguments:
- block_input: bfloat16 [256, 256, 512], P('rows', 'cols'), may hold values from -18 to 18
- norm_gain: bfloat16 [512], replicated, may hold values from 0.5 to 1.5
- saved_queries: bfloat16 [256, 256, 512], P('rows', 'cols'), may hold values from -8 to 8
- saved_keys: bfloat16 [256, 256, 512], P('rows', 'cols'), may hold values from -8 to 8
- saved_values: bfloat16 [256, 256, 512], P('rows', 'cols'), may hold values from -6 to 6
- out_grad: bfloat16 [256, 256, 512], P('rows', 'cols'), may hold values from -6 to 6
- w_query: bfloat16 [512, 512], replicated, may hold values from -0.25 to 0.25
- w_key: bfloat16 [512, 512], replicated, may hold values from -0.25 to 0.25
- w_value: bfloat16 [512, 512], replicated, may hold values from -0.25 to 0.25
- w_out: bfloat16 [512, 512], replicated, may hold values from -0.25 to 0.25
Outputs:
- block_grad: float32 [256, 256, 512], P('rows', 'cols')
The draws below stay inside these ranges and needn't reach their ends.
All inputs are finite; a program needn't handle non-finite values.
Results may differ from the reference program's by a relative error of at most 0.0044.
Values may be sent and summed in bfloat16 or wider, within the bound.
A program may use at most 128 MiB of HBM per device.

```python
import jax
import jax.numpy as jnp
from jax import lax

D = 512
HEADS = 16
GRID = 16
HEIGHT = 256
WIDTH = 256


def draw_block_input(key, part):
    key = jax.random.fold_in(key, 13)
    third = jax.random.fold_in(key, 2)
    base = jnp.clip(jax.random.normal(third, (HEIGHT, WIDTH, D), jnp.float32), -4.0, 4.0)
    return base.astype(jnp.bfloat16)


def draw_saved_queries(key, part):
    key = jax.random.fold_in(key, 11)
    base = jnp.clip(jax.random.normal(key, (HEIGHT, WIDTH, D), jnp.float32), -4.0, 4.0)
    return base.astype(jnp.bfloat16)


def draw_saved_keys(key, part):
    key = jax.random.fold_in(key, 17)
    base = jnp.clip(jax.random.normal(key, (HEIGHT, WIDTH, D), jnp.float32), -4.0, 4.0)
    return base.astype(jnp.bfloat16)


def shard_levels(key, extent, shards, smallest, top_value):
    level, own = 1.0, jax.random.fold_in(key, 6)
    for dim, parts in shards:
        steps = jnp.exp(jax.random.uniform(jax.random.fold_in(own, dim), (parts,), jnp.float32, smallest / len(shards), top_value / len(shards)))
        level = level * jnp.repeat(steps, extent[dim] // parts).reshape([-1 if axis == dim else 1 for axis in range(len(extent))])
    return level


def scatter_about(stream_key, shape, spread, limit, cuts=(), dtype=jnp.bfloat16):
    drawn = jax.random.normal(stream_key, shape, jnp.float32) * spread
    if len(cuts) > 0:
        drawn = shard_levels(stream_key, shape, cuts, -0.22, 0.18) * drawn
    return jnp.clip(drawn, min=-limit, max=limit).astype(dtype)


def setup_inputs(seed: int = 0) -> dict:
    arg_keys = jax.random.split(jax.random.key(seed), 11)
    return {
        "block_input": draw_block_input(jax.random.fold_in(arg_keys[10], 71), 0),
        "norm_gain": jnp.clip(jax.random.uniform(arg_keys[1], (D,), jnp.float32, 0.5, 1.5), 0.5, 1.5).astype(jnp.bfloat16),
        "saved_queries": draw_saved_queries(jax.random.fold_in(arg_keys[10], 71), 0),
        "saved_keys": draw_saved_keys(jax.random.fold_in(arg_keys[10], 71), 0),
        "saved_values": scatter_about(arg_keys[4], (HEIGHT, WIDTH, D), 1.0, 6.0, ((0, 8), (1, 4))),
        "out_grad": scatter_about(arg_keys[5], (HEIGHT, WIDTH, D), 1.0, 6.0, ((0, 8), (1, 4))),
        "w_query": scatter_about(arg_keys[6], (D, D), D ** -0.5, 0.25),
        "w_key": scatter_about(arg_keys[7], (D, D), D ** -0.5, 0.25),
        "w_value": scatter_about(arg_keys[8], (D, D), D ** -0.5, 0.25),
        "w_out": scatter_about(arg_keys[9], (D, D), D ** -0.5, 0.25),
    }


def rounded(value):
    return lax.optimization_barrier(value.astype(jnp.bfloat16)).astype(jnp.float32)

def window_grads(items):
    query_win, key_win, value_win, grad_win = items
    length = query_win.shape[0]
    head_dim = D // HEADS
    factor = head_dim ** (-0.5)
    query_heads = query_win.astype(jnp.float32).reshape(length, HEADS, head_dim)
    key_heads = key_win.astype(jnp.float32).reshape(length, HEADS, head_dim)
    value_heads = value_win.astype(jnp.float32).reshape(length, HEADS, head_dim)
    grad_heads = grad_win.astype(jnp.float32).reshape(length, HEADS, head_dim)
    scores = jnp.einsum('qhd,khd->hqk', query_heads, key_heads) * factor
    attention = jax.nn.softmax(scores, axis=-1)
    value_grad = jnp.einsum('hqk,qhd->khd', rounded(attention), grad_heads).astype(jnp.bfloat16)
    prob_grad = jnp.einsum('qhd,khd->hqk', grad_heads, value_heads)
    centre = lax.optimization_barrier(jnp.sum(attention * prob_grad, axis=-1, keepdims=True))
    score_grad = rounded(attention * (prob_grad - centre))
    query_grad = (jnp.einsum('hqk,khd->qhd', score_grad, key_heads) * factor).astype(jnp.bfloat16)
    key_grad = (jnp.einsum('hqk,qhd->khd', score_grad, query_heads) * factor).astype(jnp.bfloat16)
    return (query_grad.reshape(length, D), key_grad.reshape(length, D), value_grad.reshape(length, D))

def to_windows(tensor):
    row_stride = HEIGHT // GRID
    col_stride = WIDTH // GRID
    return tensor.reshape(GRID, row_stride, GRID, col_stride, D).transpose(1, 3, 0, 2, 4).reshape(row_stride * col_stride, GRID * GRID, D)

def from_windows(tensor):
    row_stride = HEIGHT // GRID
    col_stride = WIDTH // GRID
    return tensor.reshape(row_stride, col_stride, GRID, GRID, D).transpose(2, 0, 3, 1, 4).reshape(HEIGHT * WIDTH, D)

def norm_backward(block_input, norm_gain, input_grad):
    values_in = block_input.astype(jnp.float32)
    centred = values_in - lax.optimization_barrier(jnp.mean(values_in, axis=-1, keepdims=True))
    variance = lax.optimization_barrier(jnp.mean(centred * centred, axis=-1, keepdims=True))
    inv_std = lax.rsqrt(variance + 1e-05)
    normed = centred * inv_std
    scaled = input_grad.astype(jnp.float32) * norm_gain.astype(jnp.float32)
    return inv_std * (scaled - lax.optimization_barrier(jnp.mean(scaled, axis=-1, keepdims=True)) - normed * lax.optimization_barrier(jnp.mean(scaled * normed, axis=-1, keepdims=True)))

def reference(block_input, norm_gain, saved_queries, saved_keys, saved_values, out_grad, w_query, w_key, w_value, w_out):
    flat_grad = out_grad.reshape(HEIGHT * WIDTH, D)
    out_proj_grad = jnp.dot(flat_grad, w_out.T, preferred_element_type=jnp.float32).astype(jnp.bfloat16)
    query_grad, key_grad, value_grad = lax.map(window_grads, (to_windows(saved_queries), to_windows(saved_keys), to_windows(saved_values), to_windows(out_proj_grad.reshape(HEIGHT, WIDTH, D))))
    input_grad = jnp.dot(from_windows(query_grad), w_query.T, preferred_element_type=jnp.float32)
    input_grad = input_grad + jnp.dot(from_windows(key_grad), w_key.T, preferred_element_type=jnp.float32)
    input_grad = input_grad + jnp.dot(from_windows(value_grad), w_value.T, preferred_element_type=jnp.float32)
    input_grad = input_grad.astype(jnp.bfloat16)
    branch = norm_backward(block_input.reshape(HEIGHT * WIDTH, D), norm_gain, input_grad)
    return (flat_grad.astype(jnp.float32) + branch).reshape(HEIGHT, WIDTH, D)
```

```python
import functools

import jax
import jax.numpy as jnp
import numpy as np
from jax import lax
from jax.experimental import pallas as pl
from jax.experimental.pallas import tpu as pltpu
from jax.sharding import PartitionSpec as P

D = 512
HEADS = 16
GRID = 16
HEAD_DIM = D // HEADS
LANES = 128
LENGTH = GRID * GRID
FACTOR = HEAD_DIM ** (-0.5)
EXP2_FACTOR = FACTOR * float(np.log2(np.e))
MESH = pl.DeviceIdType.MESH
VMEM_BYTES = 50 * 1024 * 1024
F32 = jnp.float32
BF16 = jnp.bfloat16


def dot(left, right):
    return lax.dot_general(left, right, (((1,), (0,)), ((), ())), preferred_element_type=F32)


def dot_t(left, right):
    return lax.dot_general(left, right, (((1,), (1,)), ((), ())), preferred_element_type=F32)


def pack_kernel(perm_ref, w_out_ref, q_ref, k_ref, v_ref, g_ref, out_ref):
    chunks, _, cols, _, rows, _ = out_ref.shape
    perm = perm_ref[...]
    tokens = perm.shape[0]
    for member, ref in enumerate((q_ref, k_ref, v_ref, g_ref)):
        ordered = dot(perm, ref[...].reshape(tokens, D)).astype(BF16)
        if member == 3:
            ordered = dot_t(ordered, w_out_ref[...]).astype(BF16)
        out_ref[:, 0, :, member] = ordered.reshape(chunks, cols, rows, D)


def norm_kernel(perm_ref, gain_ref, x_ref, g_ref, back_ref, out_ref):
    perm = perm_ref[...]
    tokens = perm.shape[0]
    input_grad = dot(perm, back_ref[...].reshape(tokens, D))
    values_in = x_ref[...].reshape(tokens, D).astype(F32)
    centred = values_in - jnp.mean(values_in, axis=-1, keepdims=True)
    variance = jnp.mean(centred * centred, axis=-1, keepdims=True)
    inv_std = lax.rsqrt(variance + 1e-05)
    normed = centred * inv_std
    scaled = input_grad * gain_ref[...].astype(F32)
    branch = inv_std * (
        scaled
        - jnp.mean(scaled, axis=-1, keepdims=True)
        - normed * jnp.mean(scaled * normed, axis=-1, keepdims=True)
    )
    out_ref[...] = (g_ref[...].reshape(tokens, D).astype(F32) + branch).reshape(out_ref.shape)


def window_kernel(
    row_count, col_count, wins, part,
    send_ref, w_query_ref, w_key_ref, w_value_ref, back_ref,
    recv, reply, q_win, k_win, v_win, g_win, k_turned, dq_turned, dk_win, dv_win,
    send_sem, recv_sem, reply_sem, back_sem,
):
    chunks, devices, _, rows, _ = send_ref.shape
    my_row, my_col = lax.axis_index("rows"), lax.axis_index("cols")
    me = my_row * col_count + my_col

    def peer_of(step):
        row = lax.rem(my_row + step // col_count, row_count)
        col = lax.rem(my_col + lax.rem(step, col_count), col_count)
        return row, col, row * col_count + col

    barrier = pltpu.get_barrier_semaphore()

    @pl.loop(1, devices)
    def _(step):
        row, col, _ = peer_of(step)
        pl.semaphore_signal(barrier, inc=1, device_id=(row, col), device_id_type=MESH)

    pl.semaphore_wait(barrier, devices - 1)

    @pl.loop(0, chunks)
    def _(chunk):
        pltpu.make_async_copy(
            send_ref.at[chunk, me], recv.at[chunk, me], recv_sem.at[chunk]
        ).start()

        @pl.loop(1, devices)
        def _(step):
            row, col, index = peer_of(step)
            pltpu.make_async_remote_copy(
                src_ref=send_ref.at[chunk, index],
                dst_ref=recv.at[chunk, me],
                send_sem=send_sem.at[chunk],
                recv_sem=recv_sem.at[chunk],
                device_id=(row, col),
                device_id_type=MESH,
            ).start()

    lane_head = lax.broadcasted_iota(jnp.int32, (1, LANES), 1) // HEAD_DIM
    spread = devices * rows

    @pl.loop(0, chunks)
    def _(chunk):
        pltpu.make_async_copy(recv.at[chunk], recv.at[chunk], recv_sem.at[chunk]).wait()
        reply[chunk] = jnp.zeros((devices, rows, D), BF16)

        @pl.loop(0, wins)
        def _(win):
            slot = lax.broadcasted_iota(jnp.int32, (LENGTH, spread), 0)
            place = lax.broadcasted_iota(jnp.int32, (LENGTH, spread), 1)
            pick = (place == (slot // part) * rows + win * part + slot % part).astype(BF16)
            for member, ref in enumerate((q_win, k_win, v_win, g_win)):
                ref[...] = dot(pick, recv[chunk, :, member].reshape(spread, D)).astype(BF16)
            k_turned[...] = k_win[...].astype(F32).T.astype(BF16)

            @pl.loop(0, D // LANES)
            def _(group):
                lanes = pl.ds(pl.multiple_of(group * LANES, LANES), LANES)
                q_part, k_part = q_win[:, lanes], k_win[:, lanes]
                v_part, g_part = v_win[:, lanes], g_win[:, lanes]
                value_grad = jnp.zeros((LENGTH, LANES), F32)
                key_grad = jnp.zeros((LENGTH, LANES), F32)
                for head in range(LANES // HEAD_DIM):
                    mask = (lane_head == head).astype(BF16)
                    q_head, g_head = q_part * mask, g_part * mask
                    scores = dot_t(k_part, q_head)
                    top = jnp.max(scores, axis=0, keepdims=True)
                    weights = jnp.exp2((scores - top) * EXP2_FACTOR)
                    attention = weights * (1.0 / jnp.sum(weights, axis=0, keepdims=True))
                    value_grad += dot(attention.astype(BF16), g_head)
                    prob_grad = dot_t(v_part, g_head)
                    centre = jnp.sum(attention * prob_grad, axis=0, keepdims=True)
                    score_grad = (attention * (prob_grad - centre)).astype(BF16)
                    key_grad += dot(score_grad, q_head)
                    dims = pl.ds(pl.multiple_of(group * LANES + head * HEAD_DIM, HEAD_DIM), HEAD_DIM)
                    dq_turned[dims, :] = dot(k_turned[dims, :], score_grad) * FACTOR
                dv_win[:, lanes] = value_grad.astype(BF16)
                dk_win[:, lanes] = (key_grad * FACTOR).astype(BF16)

            total = dot_t(dq_turned[...].T.astype(BF16), w_query_ref[...])
            total += dot_t(dk_win[...], w_key_ref[...])
            total += dot_t(dv_win[...], w_value_ref[...])
            place_t = lax.broadcasted_iota(jnp.int32, (spread, LENGTH), 0)
            slot_t = lax.broadcasted_iota(jnp.int32, (spread, LENGTH), 1)
            put = (place_t == (slot_t // part) * rows + win * part + slot_t % part).astype(BF16)
            placed = dot(put, total.astype(BF16)).astype(BF16)
            reply[chunk] += placed.reshape(devices, rows, D)

        pltpu.make_async_copy(
            reply.at[chunk, me], back_ref.at[chunk, me], back_sem.at[chunk]
        ).start()

        @pl.loop(1, devices)
        def _(step):
            row, col, index = peer_of(step)
            pltpu.make_async_remote_copy(
                src_ref=reply.at[chunk, index],
                dst_ref=back_ref.at[chunk, me],
                send_sem=reply_sem.at[chunk],
                recv_sem=back_sem.at[chunk],
                device_id=(row, col),
                device_id_type=MESH,
            ).start()

    @pl.loop(0, chunks)
    def _(chunk):
        sent = send_ref.at[chunk, pl.ds(0, devices - 1)]
        pltpu.make_async_copy(sent, sent, send_sem.at[chunk]).wait()
        replied = reply.at[chunk, pl.ds(0, devices - 1)]
        pltpu.make_async_copy(replied, replied, reply_sem.at[chunk]).wait()
        pltpu.make_async_copy(back_ref.at[chunk], back_ref.at[chunk], back_sem.at[chunk]).wait()


def on_device(
    block_input,
    norm_gain,
    saved_queries,
    saved_keys,
    saved_values,
    out_grad,
    w_query,
    w_key,
    w_value,
    w_out,
):
    rows_dev, cols_dev = block_input.shape[:2]
    row_count, col_count = lax.axis_size("rows"), lax.axis_size("cols")
    devices = row_count * col_count
    row_stride = rows_dev * row_count // GRID
    col_stride = cols_dev * col_count // GRID
    row_reps, col_reps = rows_dev // row_stride, cols_dev // col_stride
    row_part, col_part = row_stride // row_count, col_stride // col_count
    windows = row_part * col_part
    part = row_reps * col_reps
    wins = next(n for n in range(1, windows + 1) if windows % n == 0 and n * part % 16 == 0)
    chunks, rows = windows // wins, wins * part

    tokens = row_reps * row_part * cols_dev
    order = (
        np.arange(tokens)
        .reshape(row_reps, row_part, col_reps, col_count, col_part)
        .transpose(1, 4, 3, 0, 2)
        .reshape(chunks, wins, col_count, part)
        .transpose(0, 2, 1, 3)
        .reshape(tokens)
    )
    perm = np.zeros((tokens, tokens), np.float32)
    perm[np.arange(tokens), order] = 1.0
    forward, backward = jnp.asarray(perm, BF16), jnp.asarray(perm.T, BF16)

    def blocks(array):
        return array.reshape(row_reps, row_stride, cols_dev, D)

    token_spec = pl.BlockSpec((row_reps, row_part, cols_dev, D), lambda r: (0, r, 0, 0))
    perm_spec = pl.BlockSpec((tokens, tokens), lambda r: (0, 0))
    weight_spec = pl.BlockSpec((D, D), lambda r: (0, 0))
    params = pltpu.CompilerParams(vmem_limit_bytes=VMEM_BYTES)

    packed = pl.pallas_call(
        pack_kernel,
        grid=(row_count,),
        in_specs=[perm_spec, weight_spec] + [token_spec] * 4,
        out_specs=pl.BlockSpec(
            (chunks, 1, col_count, 4, rows, D), lambda r: (0, r, 0, 0, 0, 0)
        ),
        out_shape=jax.ShapeDtypeStruct((chunks, row_count, col_count, 4, rows, D), BF16),
        compiler_params=params,
    )(forward, w_out, blocks(saved_queries), blocks(saved_keys), blocks(saved_values), blocks(out_grad))

    vmem = pl.BlockSpec(memory_space=pltpu.VMEM)
    hbm = pl.BlockSpec(memory_space=pl.ANY)
    window = pltpu.VMEM((LENGTH, D), BF16)
    back = pl.pallas_call(
        functools.partial(window_kernel, row_count, col_count, wins, part),
        in_specs=[hbm, vmem, vmem, vmem],
        out_specs=hbm,
        out_shape=jax.ShapeDtypeStruct((chunks, devices, rows, D), BF16),
        scratch_shapes=[
            pltpu.VMEM((chunks, devices, 4, rows, D), BF16),
            pltpu.VMEM((chunks, devices, rows, D), BF16),
            window,
            window,
            window,
            window,
            pltpu.VMEM((D, LENGTH), BF16),
            pltpu.VMEM((D, LENGTH), F32),
            window,
            window,
            pltpu.SemaphoreType.DMA((chunks,)),
            pltpu.SemaphoreType.DMA((chunks,)),
            pltpu.SemaphoreType.DMA((chunks,)),
            pltpu.SemaphoreType.DMA((chunks,)),
        ],
        compiler_params=pltpu.CompilerParams(
            collective_id=0, has_side_effects=True, vmem_limit_bytes=VMEM_BYTES
        ),
    )(packed.reshape(chunks, devices, 4, rows, D), w_query, w_key, w_value)

    result = pl.pallas_call(
        norm_kernel,
        grid=(row_count,),
        in_specs=[
            perm_spec,
            pl.BlockSpec((1, D), lambda r: (0, 0)),
            token_spec,
            token_spec,
            pl.BlockSpec((chunks, 1, col_count, rows, D), lambda r: (0, r, 0, 0, 0)),
        ],
        out_specs=token_spec,
        out_shape=jax.ShapeDtypeStruct((row_reps, row_stride, cols_dev, D), F32),
        compiler_params=params,
    )(
        backward,
        norm_gain.reshape(1, D),
        blocks(block_input),
        blocks(out_grad),
        back.reshape(chunks, row_count, col_count, rows, D),
    )
    return result.reshape(rows_dev, cols_dev, D)


def solution(mesh):
    return jax.shard_map(
        on_device,
        mesh=mesh,
        in_specs=(
            P("rows", "cols", None),
            P(),
            P("rows", "cols", None),
            P("rows", "cols", None),
            P("rows", "cols", None),
            P("rows", "cols", None),
            P(),
            P(),
            P(),
            P(),
        ),
        out_specs=P("rows", "cols", None),
        check_vma=False,
    )
```

```python
import functools

import jax
import jax.numpy as jnp
import numpy as np
from jax import lax
from jax.experimental import pallas as pl
from jax.experimental.pallas import tpu as pltpu
from jax.sharding import PartitionSpec as P

D = 512
HEADS = 16
GRID = 16
HEAD_DIM = D // HEADS
LANES = 128
LENGTH = GRID * GRID
FACTOR = HEAD_DIM ** (-0.5)
EXP2_FACTOR = FACTOR * float(np.log2(np.e))
MESH = pl.DeviceIdType.MESH
VMEM_BYTES = 50 * 1024 * 1024
WINDOW_VMEM_BYTES = 60 * 1024 * 1024
F32 = jnp.float32
BF16 = jnp.bfloat16


def dot(left, right):
    return lax.dot_general(left, right, (((1,), (0,)), ((), ())), preferred_element_type=F32)


def dot_t(left, right):
    return lax.dot_general(left, right, (((1,), (1,)), ((), ())), preferred_element_type=F32)


def norm_kernel(perm_ref, gain_ref, x_ref, g_ref, back_ref, out_ref):
    perm = perm_ref[...]
    tokens = perm.shape[0]
    input_grad = dot(perm, back_ref[...].reshape(tokens, D))
    values_in = x_ref[...].reshape(tokens, D).astype(F32)
    centred = values_in - jnp.mean(values_in, axis=-1, keepdims=True)
    variance = jnp.mean(centred * centred, axis=-1, keepdims=True)
    inv_std = lax.rsqrt(variance + 1e-05)
    normed = centred * inv_std
    scaled = input_grad * gain_ref[...].astype(F32)
    branch = inv_std * (
        scaled
        - jnp.mean(scaled, axis=-1, keepdims=True)
        - normed * jnp.mean(scaled * normed, axis=-1, keepdims=True)
    )
    out_ref[...] = (g_ref[...].reshape(tokens, D).astype(F32) + branch).reshape(out_ref.shape)


def window_kernel(
    row_count, col_count, wins, part, col_part,
    q_ref, k_ref, v_ref, g_ref, w_query_ref, w_key_ref, w_value_ref, w_out_ref, back_ref,
    stage, packed, recv, reply, weights_in, perm,
    q_win, k_win, v_win, g_win, k_turned, dq_turned, dk_win, dv_win,
    stage_sem, weight_sem, send_sem, recv_sem, reply_sem, back_sem,
):
    chunks, devices, _, rows, _ = packed.shape
    _, _, row_reps, phase_part, cols_dev, _ = stage.shape
    row_part = q_ref.shape[1] // row_count
    phases = row_part // phase_part
    phase_chunks = chunks // phases
    tokens = row_reps * phase_part * cols_dev
    steps = phases * row_count
    my_row, my_col = lax.axis_index("rows"), lax.axis_index("cols")
    me = my_row * col_count + my_col

    def peer_of(step):
        row = lax.rem(my_row + step // col_count, row_count)
        col = lax.rem(my_col + lax.rem(step, col_count), col_count)
        return row, col, row * col_count + col

    def row_of(step):
        return lax.rem(my_row + 1 + step, row_count)

    def stage_copies(step):
        slot = lax.rem(step, 2)
        first = row_of(step) * row_part + (step // row_count) * phase_part
        return [
            pltpu.make_async_copy(
                ref.at[:, pl.ds(first, phase_part)], stage.at[slot, member], stage_sem.at[slot, member]
            )
            for member, ref in enumerate((q_ref, k_ref, v_ref, g_ref))
        ]

    def send(chunk, row, col):
        index = row * col_count + col

        @pl.when(index == me)
        def _():
            pltpu.make_async_copy(
                packed.at[chunk, me], recv.at[chunk, me], recv_sem.at[chunk]
            ).start()

        @pl.when(index != me)
        def _():
            pltpu.make_async_remote_copy(
                src_ref=packed.at[chunk, index],
                dst_ref=recv.at[chunk, me],
                send_sem=send_sem.at[chunk],
                recv_sem=recv_sem.at[chunk],
                device_id=(row, col),
                device_id_type=MESH,
            ).start()

    weight_copies = [
        pltpu.make_async_copy(ref, weights_in.at[member], weight_sem.at[member])
        for member, ref in enumerate((w_out_ref, w_query_ref, w_key_ref, w_value_ref))
    ]
    for copy in stage_copies(0) + weight_copies:
        copy.start()
    barrier = pltpu.get_barrier_semaphore()

    @pl.loop(1, devices)
    def _(step):
        row, col, _ = peer_of(step)
        pl.semaphore_signal(barrier, inc=1, device_id=(row, col), device_id_type=MESH)

    target = lax.broadcasted_iota(jnp.int32, (tokens, tokens), 0)
    source = lax.broadcasted_iota(jnp.int32, (tokens, tokens), 1)
    col_reps = part // row_reps
    chunk_in, col_in = target // (col_count * rows), target // rows % col_count
    window = chunk_in * wins + target % rows // part
    row_rep, col_rep = target % part // col_reps, target % col_reps
    wanted = (row_rep * phase_part + window // col_part) * col_reps + col_rep
    wanted = (wanted * col_count + col_in) * col_part + window % col_part
    perm[...] = (source == wanted).astype(BF16)
    weight_copies[0].wait()
    pl.semaphore_wait(barrier, devices - 1)

    @pl.loop(0, steps)
    def _(step):
        @pl.when(step + 1 < steps)
        def _():
            for copy in stage_copies(step + 1):
                copy.start()

        for copy in stage_copies(step):
            copy.wait()
        slot, phase, row = lax.rem(step, 2), step // row_count, row_of(step)
        for member in range(4):
            ordered = dot(perm[...], stage[slot, member].reshape(tokens, D)).astype(BF16)
            if member == 3:
                ordered = dot_t(ordered, weights_in[0]).astype(BF16)
            packed[
                pl.ds(phase * phase_chunks, phase_chunks), pl.ds(row * col_count, col_count), member
            ] = ordered.reshape(phase_chunks, col_count, rows, D)

        @pl.when(phase == 0)
        def _():
            @pl.loop(0, col_count)
            def _(shift):
                send(0, row, lax.rem(my_col + 1 + shift, col_count))

    @pl.loop(1, chunks)
    def _(chunk):
        @pl.loop(0, devices)
        def _(step):
            row, col, _ = peer_of(step)
            send(chunk, row, col)

    for copy in weight_copies[1:]:
        copy.wait()
    lane_head = lax.broadcasted_iota(jnp.int32, (1, LANES), 1) // HEAD_DIM
    spread = devices * rows

    @pl.loop(0, chunks)
    def _(chunk):
        pltpu.make_async_copy(recv.at[chunk], recv.at[chunk], recv_sem.at[chunk]).wait()
        reply[chunk] = jnp.zeros((devices, rows, D), BF16)

        @pl.loop(0, wins)
        def _(win):
            slot = lax.broadcasted_iota(jnp.int32, (LENGTH, spread), 0)
            place = lax.broadcasted_iota(jnp.int32, (LENGTH, spread), 1)
            pick = (place == (slot // part) * rows + win * part + slot % part).astype(BF16)
            for member, ref in enumerate((q_win, k_win, v_win, g_win)):
                ref[...] = dot(pick, recv[chunk, :, member].reshape(spread, D)).astype(BF16)
            k_turned[...] = k_win[...].astype(F32).T.astype(BF16)

            @pl.loop(0, D // LANES)
            def _(group):
                lanes = pl.ds(pl.multiple_of(group * LANES, LANES), LANES)
                q_part, k_part = q_win[:, lanes], k_win[:, lanes]
                v_part, g_part = v_win[:, lanes], g_win[:, lanes]
                value_grad = jnp.zeros((LENGTH, LANES), F32)
                key_grad = jnp.zeros((LENGTH, LANES), F32)
                for head in range(LANES // HEAD_DIM):
                    mask = (lane_head == head).astype(BF16)
                    q_head, g_head = q_part * mask, g_part * mask
                    scores = dot_t(k_part, q_head)
                    top = jnp.max(scores, axis=0, keepdims=True)
                    weights = jnp.exp2((scores - top) * EXP2_FACTOR)
                    attention = weights * (1.0 / jnp.sum(weights, axis=0, keepdims=True))
                    value_grad += dot(attention.astype(BF16), g_head)
                    prob_grad = dot_t(v_part, g_head)
                    centre = jnp.sum(attention * prob_grad, axis=0, keepdims=True)
                    score_grad = (attention * (prob_grad - centre)).astype(BF16)
                    key_grad += dot(score_grad, q_head)
                    dims = pl.ds(pl.multiple_of(group * LANES + head * HEAD_DIM, HEAD_DIM), HEAD_DIM)
                    dq_turned[dims, :] = dot(k_turned[dims, :], score_grad) * FACTOR
                dv_win[:, lanes] = value_grad.astype(BF16)
                dk_win[:, lanes] = (key_grad * FACTOR).astype(BF16)

            total = dot_t(dq_turned[...].T.astype(BF16), weights_in[1])
            total += dot_t(dk_win[...], weights_in[2])
            total += dot_t(dv_win[...], weights_in[3])
            place_t = lax.broadcasted_iota(jnp.int32, (spread, LENGTH), 0)
            slot_t = lax.broadcasted_iota(jnp.int32, (spread, LENGTH), 1)
            put = (place_t == (slot_t // part) * rows + win * part + slot_t % part).astype(BF16)
            placed = dot(put, total.astype(BF16)).astype(BF16)
            reply[chunk] += placed.reshape(devices, rows, D)

        pltpu.make_async_copy(
            reply.at[chunk, me], back_ref.at[chunk, me], back_sem.at[chunk]
        ).start()

        @pl.loop(1, devices)
        def _(step):
            row, col, index = peer_of(step)
            pltpu.make_async_remote_copy(
                src_ref=reply.at[chunk, index],
                dst_ref=back_ref.at[chunk, me],
                send_sem=reply_sem.at[chunk],
                recv_sem=back_sem.at[chunk],
                device_id=(row, col),
                device_id_type=MESH,
            ).start()

    @pl.loop(0, chunks)
    def _(chunk):
        sent = packed.at[chunk, pl.ds(0, devices - 1)]
        pltpu.make_async_copy(sent, sent, send_sem.at[chunk]).wait()
        replied = reply.at[chunk, pl.ds(0, devices - 1)]
        pltpu.make_async_copy(replied, replied, reply_sem.at[chunk]).wait()
        pltpu.make_async_copy(back_ref.at[chunk], back_ref.at[chunk], back_sem.at[chunk]).wait()


def on_device(
    block_input,
    norm_gain,
    saved_queries,
    saved_keys,
    saved_values,
    out_grad,
    w_query,
    w_key,
    w_value,
    w_out,
):
    rows_dev, cols_dev = block_input.shape[:2]
    row_count, col_count = lax.axis_size("rows"), lax.axis_size("cols")
    devices = row_count * col_count
    row_stride = rows_dev * row_count // GRID
    col_stride = cols_dev * col_count // GRID
    row_reps, col_reps = rows_dev // row_stride, cols_dev // col_stride
    row_part, col_part = row_stride // row_count, col_stride // col_count
    windows = row_part * col_part
    part = row_reps * col_reps
    wins = next(n for n in range(1, windows + 1) if windows % n == 0 and n * part % 16 == 0)
    chunks, rows = windows // wins, wins * part

    phase_part = max(1, wins // col_part)
    phase_tokens = row_reps * phase_part * cols_dev
    tokens = row_reps * row_part * cols_dev
    order = (
        np.arange(tokens)
        .reshape(row_reps, row_part, col_reps, col_count, col_part)
        .transpose(1, 4, 3, 0, 2)
        .reshape(chunks, wins, col_count, part)
        .transpose(0, 2, 1, 3)
        .reshape(tokens)
    )
    perm = np.zeros((tokens, tokens), np.float32)
    perm[np.arange(tokens), order] = 1.0
    backward = jnp.asarray(perm.T, BF16)

    def blocks(array):
        return array.reshape(row_reps, row_stride, cols_dev, D)

    token_spec = pl.BlockSpec((row_reps, row_part, cols_dev, D), lambda r: (0, r, 0, 0))
    perm_spec = pl.BlockSpec((tokens, tokens), lambda r: (0, 0))
    params = pltpu.CompilerParams(vmem_limit_bytes=VMEM_BYTES)

    hbm = pl.BlockSpec(memory_space=pl.ANY)
    window = pltpu.VMEM((LENGTH, D), BF16)
    back = pl.pallas_call(
        functools.partial(window_kernel, row_count, col_count, wins, part, col_part),
        in_specs=[hbm] * 8,
        out_specs=hbm,
        out_shape=jax.ShapeDtypeStruct((chunks, devices, rows, D), BF16),
        scratch_shapes=[
            pltpu.VMEM((2, 4, row_reps, phase_part, cols_dev, D), BF16),
            pltpu.VMEM((chunks, devices, 4, rows, D), BF16),
            pltpu.VMEM((chunks, devices, 4, rows, D), BF16),
            pltpu.VMEM((chunks, devices, rows, D), BF16),
            pltpu.VMEM((4, D, D), BF16),
            pltpu.VMEM((phase_tokens, phase_tokens), BF16),
            window,
            window,
            window,
            window,
            pltpu.VMEM((D, LENGTH), BF16),
            pltpu.VMEM((D, LENGTH), F32),
            window,
            window,
            pltpu.SemaphoreType.DMA((2, 4)),
            pltpu.SemaphoreType.DMA((4,)),
            pltpu.SemaphoreType.DMA((chunks,)),
            pltpu.SemaphoreType.DMA((chunks,)),
            pltpu.SemaphoreType.DMA((chunks,)),
            pltpu.SemaphoreType.DMA((chunks,)),
        ],
        compiler_params=pltpu.CompilerParams(
            collective_id=0, has_side_effects=True, vmem_limit_bytes=WINDOW_VMEM_BYTES
        ),
    )(
        blocks(saved_queries), blocks(saved_keys), blocks(saved_values), blocks(out_grad),
        w_query, w_key, w_value, w_out,
    )

    result = pl.pallas_call(
        norm_kernel,
        grid=(row_count,),
        in_specs=[
            perm_spec,
            pl.BlockSpec((1, D), lambda r: (0, 0)),
            token_spec,
            token_spec,
            pl.BlockSpec((chunks, 1, col_count, rows, D), lambda r: (0, r, 0, 0, 0)),
        ],
        out_specs=token_spec,
        out_shape=jax.ShapeDtypeStruct((row_reps, row_stride, cols_dev, D), F32),
        compiler_params=params,
    )(
        backward,
        norm_gain.reshape(1, D),
        blocks(block_input),
        blocks(out_grad),
        back.reshape(chunks, row_count, col_count, rows, D),
    )
    return result.reshape(rows_dev, cols_dev, D)


def solution(mesh):
    return jax.shard_map(
        on_device,
        mesh=mesh,
        in_specs=(
            P("rows", "cols", None),
            P(),
            P("rows", "cols", None),
            P("rows", "cols", None),
            P("rows", "cols", None),
            P("rows", "cols", None),
            P(),
            P(),
            P(),
            P(),
        ),
        out_specs=P("rows", "cols", None),
        check_vma=False,
    )
```

```python
import functools
import math

import jax
import jax.numpy as jnp
import numpy as np
from jax import lax
from jax.experimental import pallas as pl
from jax.experimental.pallas import tpu as pltpu
from jax.sharding import PartitionSpec as P

D = 512
HEADS = 16
GRID = 16
HEAD_DIM = D // HEADS
LANES = 128
LENGTH = GRID * GRID
FACTOR = HEAD_DIM ** (-0.5)
EXP2_FACTOR = FACTOR * float(np.log2(np.e))
MESH = pl.DeviceIdType.MESH
VMEM_BYTES = 50 * 1024 * 1024
WINDOW_VMEM_BYTES = 60 * 1024 * 1024
F32 = jnp.float32
BF16 = jnp.bfloat16


def dot(left, right):
    return lax.dot_general(left, right, (((1,), (0,)), ((), ())), preferred_element_type=F32)


def dot_t(left, right):
    return lax.dot_general(left, right, (((1,), (1,)), ((), ())), preferred_element_type=F32)


def norm_kernel(perm_ref, gain_ref, x_ref, g_ref, back_ref, out_ref):
    perm = perm_ref[...]
    tokens = perm.shape[0]
    gain = gain_ref[...].astype(F32).reshape(1, D)
    fold = back_ref.shape[1]
    part = x_ref.shape[1] // fold
    for index in range(fold):
        span = slice(index * part, (index + 1) * part)
        input_grad = dot(perm, back_ref[:, index].reshape(tokens, D))
        values_in = x_ref[:, span].reshape(tokens, D).astype(F32)
        centred = values_in - jnp.mean(values_in, axis=-1, keepdims=True)
        variance = jnp.mean(centred * centred, axis=-1, keepdims=True)
        inv_std = lax.rsqrt(variance + 1e-05)
        normed = centred * inv_std
        scaled = input_grad * gain
        branch = inv_std * (
            scaled
            - jnp.mean(scaled, axis=-1, keepdims=True)
            - normed * jnp.mean(scaled * normed, axis=-1, keepdims=True)
        )
        total = g_ref[:, span].reshape(tokens, D).astype(F32) + branch
        out_ref[:, span] = total.reshape(x_ref.shape[0], part, x_ref.shape[2], D)


def window_kernel(
    row_count, col_count, wins, part, col_part,
    q_ref, k_ref, v_ref, g_ref, w_query_ref, w_key_ref, w_value_ref, w_out_ref, back_ref,
    stage, packed, recv, reply, weights_in, perm,
    q_win, k_win, v_win, g_win, k_turned, dq_turned, dk_win, dv_win,
    stage_sem, weight_sem, send_sem, recv_sem, reply_sem, back_sem,
):
    chunks, devices, _, rows, _ = packed.shape
    _, _, row_reps, phase_part, cols_dev, _ = stage.shape
    row_part = q_ref.shape[1] // row_count
    phases = row_part // phase_part
    phase_chunks = chunks // phases
    tokens = row_reps * phase_part * cols_dev
    steps = phases * row_count
    my_row, my_col = lax.axis_index("rows"), lax.axis_index("cols")
    me = my_row * col_count + my_col

    def peer_of(step):
        row = lax.rem(my_row + step // col_count, row_count)
        col = lax.rem(my_col + lax.rem(step, col_count), col_count)
        return row, col, row * col_count + col

    def row_of(step):
        return lax.rem(my_row + 1 + step, row_count)

    def stage_copies(step):
        slot = lax.rem(step, 2)
        first = row_of(step) * row_part + (step // row_count) * phase_part
        return [
            pltpu.make_async_copy(
                ref.at[:, pl.ds(first, phase_part)], stage.at[slot, member], stage_sem.at[slot, member]
            )
            for member, ref in enumerate((q_ref, k_ref, v_ref, g_ref))
        ]

    def send(chunk, row, col):
        index = row * col_count + col

        @pl.when(index == me)
        def _():
            pltpu.make_async_copy(
                packed.at[chunk, me], recv.at[chunk, me], recv_sem.at[chunk]
            ).start()

        @pl.when(index != me)
        def _():
            pltpu.make_async_remote_copy(
                src_ref=packed.at[chunk, index],
                dst_ref=recv.at[chunk, me],
                send_sem=send_sem.at[chunk],
                recv_sem=recv_sem.at[chunk],
                device_id=(row, col),
                device_id_type=MESH,
            ).start()

    weight_copies = [
        pltpu.make_async_copy(ref, weights_in.at[member], weight_sem.at[member])
        for member, ref in enumerate((w_out_ref, w_query_ref, w_key_ref, w_value_ref))
    ]
    for copy in stage_copies(0) + weight_copies:
        copy.start()
    barrier = pltpu.get_barrier_semaphore()

    @pl.loop(1, devices)
    def _(step):
        row, col, _ = peer_of(step)
        pl.semaphore_signal(barrier, inc=1, device_id=(row, col), device_id_type=MESH)

    target = lax.broadcasted_iota(jnp.int32, (tokens, tokens), 0)
    source = lax.broadcasted_iota(jnp.int32, (tokens, tokens), 1)
    col_reps = part // row_reps
    chunk_in, col_in = target // (col_count * rows), target // rows % col_count
    window = chunk_in * wins + target % rows // part
    row_rep, col_rep = target % part // col_reps, target % col_reps
    wanted = (row_rep * phase_part + window // col_part) * col_reps + col_rep
    wanted = (wanted * col_count + col_in) * col_part + window % col_part
    perm[...] = (source == wanted).astype(BF16)
    weight_copies[0].wait()
    pl.semaphore_wait(barrier, devices - 1)

    @pl.loop(0, steps)
    def _(step):
        @pl.when(step + 1 < steps)
        def _():
            for copy in stage_copies(step + 1):
                copy.start()

        for copy in stage_copies(step):
            copy.wait()
        slot, phase, row = lax.rem(step, 2), step // row_count, row_of(step)
        for member in range(4):
            ordered = dot(perm[...], stage[slot, member].reshape(tokens, D)).astype(BF16)
            if member == 3:
                ordered = dot_t(ordered, weights_in[0]).astype(BF16)
            packed[
                pl.ds(phase * phase_chunks, phase_chunks), pl.ds(row * col_count, col_count), member
            ] = ordered.reshape(phase_chunks, col_count, rows, D)

        @pl.when(phase == 0)
        def _():
            @pl.loop(0, col_count)
            def _(shift):
                send(0, row, lax.rem(my_col + 1 + shift, col_count))

    @pl.loop(1, chunks)
    def _(chunk):
        @pl.loop(0, devices)
        def _(step):
            row, col, _ = peer_of(step)
            send(chunk, row, col)

    for copy in weight_copies[1:]:
        copy.wait()
    lane_head = lax.broadcasted_iota(jnp.int32, (1, LANES), 1) // HEAD_DIM
    spread = devices * rows

    @pl.loop(0, chunks)
    def _(chunk):
        pltpu.make_async_copy(recv.at[chunk], recv.at[chunk], recv_sem.at[chunk]).wait()
        reply[chunk] = jnp.zeros((devices, rows, D), BF16)

        @pl.loop(0, wins)
        def _(win):
            slot = lax.broadcasted_iota(jnp.int32, (LENGTH, spread), 0)
            place = lax.broadcasted_iota(jnp.int32, (LENGTH, spread), 1)
            pick = (place == (slot // part) * rows + win * part + slot % part).astype(BF16)
            for member, ref in enumerate((q_win, k_win, v_win, g_win)):
                ref[...] = dot(pick, recv[chunk, :, member].reshape(spread, D)).astype(BF16)
            k_turned[...] = k_win[...].astype(F32).T.astype(BF16)

            @pl.loop(0, D // LANES)
            def _(group):
                lanes = pl.ds(pl.multiple_of(group * LANES, LANES), LANES)
                q_part, k_part = q_win[:, lanes], k_win[:, lanes]
                v_part, g_part = v_win[:, lanes], g_win[:, lanes]
                value_grad = jnp.zeros((LENGTH, LANES), F32)
                key_grad = jnp.zeros((LENGTH, LANES), F32)
                for head in range(LANES // HEAD_DIM):
                    mask = (lane_head == head).astype(BF16)
                    q_head, g_head = q_part * mask, g_part * mask
                    scores = dot_t(k_part, q_head)
                    top = jnp.max(scores, axis=0, keepdims=True)
                    weights = jnp.exp2((scores - top) * EXP2_FACTOR)
                    attention = weights * (1.0 / jnp.sum(weights, axis=0, keepdims=True))
                    value_grad += dot(attention.astype(BF16), g_head)
                    prob_grad = dot_t(v_part, g_head)
                    centre = jnp.sum(attention * prob_grad, axis=0, keepdims=True)
                    score_grad = (attention * (prob_grad - centre)).astype(BF16)
                    key_grad += dot(score_grad, q_head)
                    dims = pl.ds(pl.multiple_of(group * LANES + head * HEAD_DIM, HEAD_DIM), HEAD_DIM)
                    dq_turned[dims, :] = dot(k_turned[dims, :], score_grad) * FACTOR
                dv_win[:, lanes] = value_grad.astype(BF16)
                dk_win[:, lanes] = (key_grad * FACTOR).astype(BF16)

            total = dot_t(dq_turned[...].T.astype(BF16), weights_in[1])
            total += dot_t(dk_win[...], weights_in[2])
            total += dot_t(dv_win[...], weights_in[3])
            place_t = lax.broadcasted_iota(jnp.int32, (spread, LENGTH), 0)
            slot_t = lax.broadcasted_iota(jnp.int32, (spread, LENGTH), 1)
            put = (place_t == (slot_t // part) * rows + win * part + slot_t % part).astype(BF16)
            placed = dot(put, total.astype(BF16)).astype(BF16)
            reply[chunk] += placed.reshape(devices, rows, D)

        pltpu.make_async_copy(
            reply.at[chunk, me], back_ref.at[chunk, me], back_sem.at[chunk]
        ).start()

        @pl.loop(1, devices)
        def _(step):
            row, col, index = peer_of(step)
            pltpu.make_async_remote_copy(
                src_ref=reply.at[chunk, index],
                dst_ref=back_ref.at[chunk, me],
                send_sem=reply_sem.at[chunk],
                recv_sem=back_sem.at[chunk],
                device_id=(row, col),
                device_id_type=MESH,
            ).start()

    @pl.loop(0, chunks)
    def _(chunk):
        sent = packed.at[chunk, pl.ds(0, devices - 1)]
        pltpu.make_async_copy(sent, sent, send_sem.at[chunk]).wait()
        replied = reply.at[chunk, pl.ds(0, devices - 1)]
        pltpu.make_async_copy(replied, replied, reply_sem.at[chunk]).wait()
        pltpu.make_async_copy(back_ref.at[chunk], back_ref.at[chunk], back_sem.at[chunk]).wait()


def on_device(
    block_input,
    norm_gain,
    saved_queries,
    saved_keys,
    saved_values,
    out_grad,
    w_query,
    w_key,
    w_value,
    w_out,
):
    rows_dev, cols_dev = block_input.shape[:2]
    row_count, col_count = lax.axis_size("rows"), lax.axis_size("cols")
    devices = row_count * col_count
    row_stride = rows_dev * row_count // GRID
    col_stride = cols_dev * col_count // GRID
    row_reps, col_reps = rows_dev // row_stride, cols_dev // col_stride
    row_part, col_part = row_stride // row_count, col_stride // col_count
    windows = row_part * col_part
    part = row_reps * col_reps
    wins = next(n for n in range(1, windows + 1) if windows % n == 0 and n * part % 16 == 0)
    chunks, rows = windows // wins, wins * part

    phase_part = max(1, wins // col_part)
    phase_tokens = row_reps * phase_part * cols_dev
    tokens = row_reps * row_part * cols_dev
    order = (
        np.arange(tokens)
        .reshape(row_reps, row_part, col_reps, col_count, col_part)
        .transpose(1, 4, 3, 0, 2)
        .reshape(chunks, wins, col_count, part)
        .transpose(0, 2, 1, 3)
        .reshape(tokens)
    )
    perm = np.zeros((tokens, tokens), np.float32)
    perm[np.arange(tokens), order] = 1.0
    backward = jnp.asarray(perm.T, BF16)

    def blocks(array):
        return array.reshape(row_reps, row_stride, cols_dev, D)

    fold = math.gcd(row_count, 2)
    token_spec = pl.BlockSpec((row_reps, fold * row_part, cols_dev, D), lambda r: (0, r, 0, 0))
    perm_spec = pl.BlockSpec((tokens, tokens), lambda r: (0, 0))
    params = pltpu.CompilerParams(vmem_limit_bytes=VMEM_BYTES)

    hbm = pl.BlockSpec(memory_space=pl.ANY)
    window = pltpu.VMEM((LENGTH, D), BF16)
    back = pl.pallas_call(
        functools.partial(window_kernel, row_count, col_count, wins, part, col_part),
        in_specs=[hbm] * 8,
        out_specs=hbm,
        out_shape=jax.ShapeDtypeStruct((chunks, devices, rows, D), BF16),
        scratch_shapes=[
            pltpu.VMEM((2, 4, row_reps, phase_part, cols_dev, D), BF16),
            pltpu.VMEM((chunks, devices, 4, rows, D), BF16),
            pltpu.VMEM((chunks, devices, 4, rows, D), BF16),
            pltpu.VMEM((chunks, devices, rows, D), BF16),
            pltpu.VMEM((4, D, D), BF16),
            pltpu.VMEM((phase_tokens, phase_tokens), BF16),
            window,
            window,
            window,
            window,
            pltpu.VMEM((D, LENGTH), BF16),
            pltpu.VMEM((D, LENGTH), F32),
            window,
            window,
            pltpu.SemaphoreType.DMA((2, 4)),
            pltpu.SemaphoreType.DMA((4,)),
            pltpu.SemaphoreType.DMA((chunks,)),
            pltpu.SemaphoreType.DMA((chunks,)),
            pltpu.SemaphoreType.DMA((chunks,)),
            pltpu.SemaphoreType.DMA((chunks,)),
        ],
        compiler_params=pltpu.CompilerParams(
            collective_id=0, has_side_effects=True, vmem_limit_bytes=WINDOW_VMEM_BYTES
        ),
    )(
        blocks(saved_queries), blocks(saved_keys), blocks(saved_values), blocks(out_grad),
        w_query, w_key, w_value, w_out,
    )

    result = pl.pallas_call(
        norm_kernel,
        grid=(row_count // fold,),
        in_specs=[
            perm_spec,
            pl.BlockSpec((D,), lambda r: (0,)),
            token_spec,
            token_spec,
            pl.BlockSpec((chunks, fold, col_count, rows, D), lambda r: (0, r, 0, 0, 0)),
        ],
        out_specs=token_spec,
        out_shape=jax.ShapeDtypeStruct((row_reps, row_stride, cols_dev, D), F32),
        compiler_params=params,
    )(
        backward,
        norm_gain,
        blocks(block_input),
        blocks(out_grad),
        back.reshape(chunks, row_count, col_count, rows, D),
    )
    return result.reshape(rows_dev, cols_dev, D)


def solution(mesh):
    return jax.shard_map(
        on_device,
        mesh=mesh,
        in_specs=(
            P("rows", "cols", None),
            P(),
            P("rows", "cols", None),
            P("rows", "cols", None),
            P("rows", "cols", None),
            P("rows", "cols", None),
            P(),
            P(),
            P(),
            P(),
        ),
        out_specs=P("rows", "cols", None),
        check_vma=False,
    )
```

```python
import functools
import math

import jax
import jax.numpy as jnp
import numpy as np
from jax import lax
from jax.experimental import pallas as pl
from jax.experimental.pallas import tpu as pltpu
from jax.sharding import PartitionSpec as P

D = 512
HEADS = 16
GRID = 16
HEAD_DIM = D // HEADS
LANES = 128
LENGTH = GRID * GRID
FACTOR = HEAD_DIM ** (-0.5)
EXP2_FACTOR = FACTOR * float(np.log2(np.e))
MESH = pl.DeviceIdType.MESH
VMEM_BYTES = 50 * 1024 * 1024
WINDOW_VMEM_BYTES = 60 * 1024 * 1024
F32 = jnp.float32
BF16 = jnp.bfloat16


def dot(left, right):
    return lax.dot_general(left, right, (((1,), (0,)), ((), ())), preferred_element_type=F32)


def dot_t(left, right):
    return lax.dot_general(left, right, (((1,), (1,)), ((), ())), preferred_element_type=F32)


def norm_kernel(perm_ref, gain_ref, x_ref, g_ref, back_ref, out_ref):
    perm = perm_ref[...]
    tokens = perm.shape[0]
    gain = gain_ref[...].astype(F32).reshape(1, D)
    fold = back_ref.shape[1]
    part = x_ref.shape[1] // fold
    for index in range(fold):
        span = slice(index * part, (index + 1) * part)
        input_grad = dot(perm, back_ref[:, index].reshape(tokens, D))
        values_in = x_ref[:, span].reshape(tokens, D).astype(F32)
        centred = values_in - jnp.mean(values_in, axis=-1, keepdims=True)
        variance = jnp.mean(centred * centred, axis=-1, keepdims=True)
        inv_std = lax.rsqrt(variance + 1e-05)
        scaled = input_grad * gain
        slope = inv_std * inv_std * jnp.mean(scaled * centred, axis=-1, keepdims=True)
        branch = inv_std * (scaled - jnp.mean(scaled, axis=-1, keepdims=True) - centred * slope)
        total = g_ref[:, span].reshape(tokens, D).astype(F32) + branch
        out_ref[:, span] = total.reshape(x_ref.shape[0], part, x_ref.shape[2], D)


def window_kernel(
    row_count, col_count, wins, part, col_part,
    q_ref, k_ref, v_ref, g_ref, w_query_ref, w_key_ref, w_value_ref, w_out_ref, back_ref,
    stage, packed, recv, reply, weights_in, perm,
    q_win, k_win, v_win, g_win, k_turned, dq_turned, dk_win, dv_win,
    stage_sem, weight_sem, send_sem, recv_sem, reply_sem, back_sem,
):
    chunks, devices, _, rows, _ = packed.shape
    _, _, row_reps, phase_part, cols_dev, _ = stage.shape
    row_part = q_ref.shape[1] // row_count
    phases = row_part // phase_part
    phase_chunks = chunks // phases
    tokens = row_reps * phase_part * cols_dev
    steps = phases * row_count
    my_row, my_col = lax.axis_index("rows"), lax.axis_index("cols")
    me = my_row * col_count + my_col

    def peer_of(step):
        row = lax.rem(my_row + step // col_count, row_count)
        col = lax.rem(my_col + lax.rem(step, col_count), col_count)
        return row, col, row * col_count + col

    def row_of(step):
        return lax.rem(my_row + 1 + step, row_count)

    def stage_copies(step):
        slot = lax.rem(step, 2)
        first = row_of(step) * row_part + (step // row_count) * phase_part
        return [
            pltpu.make_async_copy(
                ref.at[:, pl.ds(first, phase_part)], stage.at[slot, member], stage_sem.at[slot, member]
            )
            for member, ref in enumerate((q_ref, k_ref, v_ref, g_ref))
        ]

    def send(chunk, row, col):
        index = row * col_count + col

        @pl.when(index == me)
        def _():
            pltpu.make_async_copy(
                packed.at[chunk, me], recv.at[chunk, me], recv_sem.at[chunk]
            ).start()

        @pl.when(index != me)
        def _():
            pltpu.make_async_remote_copy(
                src_ref=packed.at[chunk, index],
                dst_ref=recv.at[chunk, me],
                send_sem=send_sem.at[chunk],
                recv_sem=recv_sem.at[chunk],
                device_id=(row, col),
                device_id_type=MESH,
            ).start()

    weight_copies = [
        pltpu.make_async_copy(ref, weights_in.at[member], weight_sem.at[member])
        for member, ref in enumerate((w_out_ref, w_query_ref, w_key_ref, w_value_ref))
    ]
    for copy in stage_copies(0) + weight_copies:
        copy.start()
    barrier = pltpu.get_barrier_semaphore()

    @pl.loop(1, devices)
    def _(step):
        row, col, _ = peer_of(step)
        pl.semaphore_signal(barrier, inc=1, device_id=(row, col), device_id_type=MESH)

    target = lax.broadcasted_iota(jnp.int32, (tokens, tokens), 0)
    source = lax.broadcasted_iota(jnp.int32, (tokens, tokens), 1)
    col_reps = part // row_reps
    chunk_in, col_in = target // (col_count * rows), target // rows % col_count
    window = chunk_in * wins + target % rows // part
    row_rep, col_rep = target % part // col_reps, target % col_reps
    wanted = (row_rep * phase_part + window // col_part) * col_reps + col_rep
    wanted = (wanted * col_count + col_in) * col_part + window % col_part
    perm[...] = (source == wanted).astype(BF16)
    weight_copies[0].wait()
    pl.semaphore_wait(barrier, devices - 1)

    @pl.loop(0, steps)
    def _(step):
        @pl.when(step + 1 < steps)
        def _():
            for copy in stage_copies(step + 1):
                copy.start()

        for copy in stage_copies(step):
            copy.wait()
        slot, phase, row = lax.rem(step, 2), step // row_count, row_of(step)
        for member in range(4):
            ordered = dot(perm[...], stage[slot, member].reshape(tokens, D)).astype(BF16)
            if member == 3:
                ordered = dot_t(ordered, weights_in[0]).astype(BF16)
            packed[
                pl.ds(phase * phase_chunks, phase_chunks), pl.ds(row * col_count, col_count), member
            ] = ordered.reshape(phase_chunks, col_count, rows, D)

        @pl.when(phase == 0)
        def _():
            @pl.loop(0, col_count)
            def _(shift):
                send(0, row, lax.rem(my_col + 1 + shift, col_count))

    @pl.loop(1, chunks)
    def _(chunk):
        @pl.loop(0, devices)
        def _(step):
            row, col, _ = peer_of(step)
            send(chunk, row, col)

    for copy in weight_copies[1:]:
        copy.wait()
    lane_head = lax.broadcasted_iota(jnp.int32, (1, LANES), 1) // HEAD_DIM
    spread = devices * rows

    @pl.loop(0, chunks)
    def _(chunk):
        pltpu.make_async_copy(recv.at[chunk], recv.at[chunk], recv_sem.at[chunk]).wait()
        reply[chunk] = jnp.zeros((devices, rows, D), BF16)

        @pl.loop(0, wins)
        def _(win):
            slot = lax.broadcasted_iota(jnp.int32, (LENGTH, spread), 0)
            place = lax.broadcasted_iota(jnp.int32, (LENGTH, spread), 1)
            pick = (place == (slot // part) * rows + win * part + slot % part).astype(BF16)
            for member, ref in enumerate((q_win, k_win, v_win, g_win)):
                ref[...] = dot(pick, recv[chunk, :, member].reshape(spread, D)).astype(BF16)
            k_turned[...] = k_win[...].astype(F32).T.astype(BF16)

            @pl.loop(0, D // LANES)
            def _(group):
                lanes = pl.ds(pl.multiple_of(group * LANES, LANES), LANES)
                q_part, k_part = q_win[:, lanes], k_win[:, lanes]
                v_part, g_part = v_win[:, lanes], g_win[:, lanes]
                value_grad = jnp.zeros((LENGTH, LANES), F32)
                key_grad = jnp.zeros((LENGTH, LANES), F32)
                for head in range(LANES // HEAD_DIM):
                    mask = (lane_head == head).astype(BF16)
                    q_head, g_head = q_part * mask, g_part * mask
                    scores = dot_t(k_part, q_head)
                    top = jnp.max(scores, axis=0, keepdims=True)
                    weights = jnp.exp2((scores - top) * EXP2_FACTOR)
                    attention = weights * (1.0 / jnp.sum(weights, axis=0, keepdims=True))
                    value_grad += dot(attention.astype(BF16), g_head)
                    prob_grad = dot_t(v_part, g_head)
                    centre = jnp.sum(attention * prob_grad, axis=0, keepdims=True)
                    score_grad = (attention * (prob_grad - centre)).astype(BF16)
                    key_grad += dot(score_grad, q_head)
                    dims = pl.ds(pl.multiple_of(group * LANES + head * HEAD_DIM, HEAD_DIM), HEAD_DIM)
                    dq_turned[dims, :] = dot(k_turned[dims, :], score_grad) * FACTOR
                dv_win[:, lanes] = value_grad.astype(BF16)
                dk_win[:, lanes] = (key_grad * FACTOR).astype(BF16)

            total = dot_t(dq_turned[...].T.astype(BF16), weights_in[1])
            total += dot_t(dk_win[...], weights_in[2])
            total += dot_t(dv_win[...], weights_in[3])
            place_t = lax.broadcasted_iota(jnp.int32, (spread, LENGTH), 0)
            slot_t = lax.broadcasted_iota(jnp.int32, (spread, LENGTH), 1)
            put = (place_t == (slot_t // part) * rows + win * part + slot_t % part).astype(BF16)
            placed = dot(put, total.astype(BF16)).astype(BF16)
            reply[chunk] += placed.reshape(devices, rows, D)

        pltpu.make_async_copy(
            reply.at[chunk, me], back_ref.at[chunk, me], back_sem.at[chunk]
        ).start()

        @pl.loop(1, devices)
        def _(step):
            row, col, index = peer_of(step)
            pltpu.make_async_remote_copy(
                src_ref=reply.at[chunk, index],
                dst_ref=back_ref.at[chunk, me],
                send_sem=reply_sem.at[chunk],
                recv_sem=back_sem.at[chunk],
                device_id=(row, col),
                device_id_type=MESH,
            ).start()

    @pl.loop(0, chunks)
    def _(chunk):
        sent = packed.at[chunk, pl.ds(0, devices - 1)]
        pltpu.make_async_copy(sent, sent, send_sem.at[chunk]).wait()
        replied = reply.at[chunk, pl.ds(0, devices - 1)]
        pltpu.make_async_copy(replied, replied, reply_sem.at[chunk]).wait()
        pltpu.make_async_copy(back_ref.at[chunk], back_ref.at[chunk], back_sem.at[chunk]).wait()


def on_device(
    block_input,
    norm_gain,
    saved_queries,
    saved_keys,
    saved_values,
    out_grad,
    w_query,
    w_key,
    w_value,
    w_out,
):
    rows_dev, cols_dev = block_input.shape[:2]
    row_count, col_count = lax.axis_size("rows"), lax.axis_size("cols")
    devices = row_count * col_count
    row_stride = rows_dev * row_count // GRID
    col_stride = cols_dev * col_count // GRID
    row_reps, col_reps = rows_dev // row_stride, cols_dev // col_stride
    row_part, col_part = row_stride // row_count, col_stride // col_count
    windows = row_part * col_part
    part = row_reps * col_reps
    wins = next(n for n in range(1, windows + 1) if windows % n == 0 and n * part % 16 == 0)
    chunks, rows = windows // wins, wins * part

    phase_part = max(1, wins // col_part)
    phase_tokens = row_reps * phase_part * cols_dev
    tokens = row_reps * row_part * cols_dev
    order = (
        np.arange(tokens)
        .reshape(row_reps, row_part, col_reps, col_count, col_part)
        .transpose(1, 4, 3, 0, 2)
        .reshape(chunks, wins, col_count, part)
        .transpose(0, 2, 1, 3)
        .reshape(tokens)
    )
    perm = np.zeros((tokens, tokens), np.float32)
    perm[np.arange(tokens), order] = 1.0
    backward = jnp.asarray(perm.T, BF16)

    def blocks(array):
        return array.reshape(row_reps, row_stride, cols_dev, D)

    fold = math.gcd(row_count, 4)
    token_spec = pl.BlockSpec((row_reps, fold * row_part, cols_dev, D), lambda r: (0, r, 0, 0))
    perm_spec = pl.BlockSpec((tokens, tokens), lambda r: (0, 0))
    params = pltpu.CompilerParams(vmem_limit_bytes=VMEM_BYTES)

    hbm = pl.BlockSpec(memory_space=pl.ANY)
    window = pltpu.VMEM((LENGTH, D), BF16)
    back = pl.pallas_call(
        functools.partial(window_kernel, row_count, col_count, wins, part, col_part),
        in_specs=[hbm] * 8,
        out_specs=hbm,
        out_shape=jax.ShapeDtypeStruct((chunks, devices, rows, D), BF16),
        scratch_shapes=[
            pltpu.VMEM((2, 4, row_reps, phase_part, cols_dev, D), BF16),
            pltpu.VMEM((chunks, devices, 4, rows, D), BF16),
            pltpu.VMEM((chunks, devices, 4, rows, D), BF16),
            pltpu.VMEM((chunks, devices, rows, D), BF16),
            pltpu.VMEM((4, D, D), BF16),
            pltpu.VMEM((phase_tokens, phase_tokens), BF16),
            window,
            window,
            window,
            window,
            pltpu.VMEM((D, LENGTH), BF16),
            pltpu.VMEM((D, LENGTH), F32),
            window,
            window,
            pltpu.SemaphoreType.DMA((2, 4)),
            pltpu.SemaphoreType.DMA((4,)),
            pltpu.SemaphoreType.DMA((chunks,)),
            pltpu.SemaphoreType.DMA((chunks,)),
            pltpu.SemaphoreType.DMA((chunks,)),
            pltpu.SemaphoreType.DMA((chunks,)),
        ],
        compiler_params=pltpu.CompilerParams(
            collective_id=0, has_side_effects=True, vmem_limit_bytes=WINDOW_VMEM_BYTES
        ),
    )(
        blocks(saved_queries), blocks(saved_keys), blocks(saved_values), blocks(out_grad),
        w_query, w_key, w_value, w_out,
    )

    result = pl.pallas_call(
        norm_kernel,
        grid=(row_count // fold,),
        in_specs=[
            perm_spec,
            pl.BlockSpec((D,), lambda r: (0,)),
            token_spec,
            token_spec,
            pl.BlockSpec((chunks, fold, col_count, rows, D), lambda r: (0, r, 0, 0, 0)),
        ],
        out_specs=token_spec,
        out_shape=jax.ShapeDtypeStruct((row_reps, row_stride, cols_dev, D), F32),
        compiler_params=params,
    )(
        backward,
        norm_gain,
        blocks(block_input),
        blocks(out_grad),
        back.reshape(chunks, row_count, col_count, rows, D),
    )
    return result.reshape(rows_dev, cols_dev, D)


def solution(mesh):
    return jax.shard_map(
        on_device,
        mesh=mesh,
        in_specs=(
            P("rows", "cols", None),
            P(),
            P("rows", "cols", None),
            P("rows", "cols", None),
            P("rows", "cols", None),
            P("rows", "cols", None),
            P(),
            P(),
            P(),
            P(),
        ),
        out_specs=P("rows", "cols", None),
        check_vma=False,
    )
```
